768 devices in a mesh: dp: 24 (over y_hi, z), tensor: 32 (over x, y_lo, core).
Axes of the slice: x: 4, y: 8 (y_hi: 2, y_lo: 4; y = y_hi * 4 + y_lo), z: 12, core: 2. Of those that a mesh axis runs over, the one named last changes fastest.
Arguments:
- tokens: bfloat16 [192, 12288], P('tensor', 'dp'), may hold values from -6 to 6
- gate_weight: bfloat16 [12288, 28672], P('dp', 'tensor'), may hold values from -0.0546875 to 0.0546875
- up_weight: bfloat16 [12288, 28672], P('dp', 'tensor'), may hold values from -0.0546875 to 0.0546875
- down_weight: bfloat16 [28672, 12288], P('tensor', 'dp'), may hold values from -0.03125 to 0.03125
- out_grad: bfloat16 [192, 12288], P('tensor', 'dp'), may hold values from -0.29882812 to 0.29882812
Outputs:
- mixed: bfloat16 [192, 12288], P('tensor', 'dp')
- down_grad: bfloat16 [28672, 12288], P('tensor', 'dp')
The draws below stay inside these ranges and needn't reach their ends.
All inputs are finite; a program needn't handle non-finite values.
Results may differ from the reference program's by a relative error of at most 0.0049.
Values may be sent and summed in bfloat16 or wider, within the bound.
No kernel may reach another device: no remote copies, remote signals or barrier semaphores. Data moves between devices by JAX's collectives and lax.ppermute only.
A program may use at most 32 MiB of HBM per device.

```python
import jax
import jax.numpy as jnp
from jax import lax

D = 12288
FF = 28672
TOKENS = 192


def shard_levels(key, extent, split, low, largest):
    factor_of, own = 1.0, jax.random.fold_in(key, 6)
    for position, blocks in split:
        draws = jnp.exp(jax.random.uniform(jax.random.fold_in(own, position), (blocks,), jnp.float32, low / len(split), largest / len(split)))
        factor_of = factor_of * jnp.repeat(draws, extent[position] // blocks).reshape([-1 if axis == position else 1 for axis in range(len(extent))])
    return factor_of


def bell_draw(stream_key, dims, width, limit, pieces=(), kind=jnp.bfloat16):
    array = width * jax.random.normal(stream_key, dims, jnp.float32)
    if pieces:
        array = array * shard_levels(stream_key, dims, pieces, -0.22, 0.18)
    return jnp.clip(array, -limit, limit).astype(kind)


def setup_inputs(seed: int = 0) -> dict:
    arg_keys = jax.random.split(jax.random.key(seed), 6)
    tokens = bell_draw(arg_keys[0], (TOKENS, D), 1.0, 6.0, ((0, 32), (1, 24)))
    gate_weight = bell_draw(arg_keys[1], (D, FF), D ** -0.5, 0.0546875, ((0, 24), (1, 32)))
    up_weight = bell_draw(arg_keys[2], (D, FF), D ** -0.5, 0.0546875, ((0, 24), (1, 32)))
    down_weight = bell_draw(arg_keys[3], (FF, D), FF ** -0.5, 0.03125, ((0, 32), (1, 24)))
    out_grad = bell_draw(arg_keys[4], (TOKENS, D), 0.05, 0.29882812, ((0, 32), (1, 24)))
    return {"tokens": tokens, "gate_weight": gate_weight, "up_weight": up_weight, "down_weight": down_weight, "out_grad": out_grad}


def reference(tokens, gate_weight, up_weight, down_weight, out_grad):
    gate_values = jnp.dot(tokens, gate_weight, preferred_element_type=jnp.float32)
    up_values = jnp.dot(tokens, up_weight, preferred_element_type=jnp.float32)
    hidden = (jax.nn.silu(gate_values) * up_values).astype(jnp.bfloat16)
    mixed = jnp.dot(hidden, down_weight, preferred_element_type=jnp.float32).astype(jnp.bfloat16)
    down_grad = lax.dot_general(hidden, out_grad, (((0,), (0,)), ((), ())), preferred_element_type=jnp.float32)
    return mixed, down_grad.astype(jnp.bfloat16)
```

```python
import jax
import jax.numpy as jnp
from jax import lax
from jax.sharding import PartitionSpec as P


def gather_rows(block, axis):
    size = lax.axis_size(axis)
    copies = jnp.broadcast_to(block[None], (size, *block.shape))
    return lax.all_to_all(copies, axis, 0, 0, tiled=True)


def activate(summed, hidden_width):
    gate_values = summed[:, :hidden_width]
    up_values = summed[:, hidden_width:]
    return (jax.nn.silu(gate_values) * up_values).astype(jnp.bfloat16)


def body(tokens, gate_weight, up_weight, down_weight, out_grad):
    hidden_width = gate_weight.shape[1]
    own_rows, width = tokens.shape
    dp, tensor = lax.axis_size("dp"), lax.axis_size("tensor")
    rows = own_rows * tensor
    with jax.named_scope("gather_tokens"):
        both = gather_rows(jnp.stack([tokens, out_grad]), "tensor")
        gathered = both[:, 0].reshape(rows, width)
        cotangent = both[:, 1].reshape(rows, width)
    with jax.named_scope("gate_up_partial"):
        paired = jnp.concatenate([gate_weight, up_weight], axis=1)
        partial = jnp.dot(gathered, paired, preferred_element_type=jnp.float32)
    with jax.named_scope("gate_up_exchange"):
        parts = lax.all_to_all(partial.reshape(dp, rows // dp, -1), "dp", 0, 0, tiled=True)
    with jax.named_scope("activation"):
        hidden_share = activate(parts.sum(axis=0), hidden_width)
    with jax.named_scope("gather_hidden"):
        hidden = gather_rows(hidden_share, "dp").reshape(rows, hidden_width)
    with jax.named_scope("down"):
        mixed_partial = jnp.dot(hidden, down_weight, preferred_element_type=jnp.float32)
    with jax.named_scope("mixed_exchange"):
        mixed_parts = lax.all_to_all(
            mixed_partial.reshape(tensor, own_rows, width), "tensor", 0, 0, tiled=True
        )
        mixed = mixed_parts.sum(axis=0).astype(jnp.bfloat16)
    with jax.named_scope("down_grad"):
        contract = (((0,), (0,)), ((), ()))
        down_grad = lax.dot_general(hidden, cotangent, contract, preferred_element_type=jnp.float32)
    return (mixed, down_grad.astype(jnp.bfloat16))


def solution(mesh):
    placed = (
        P("tensor", "dp"),
        P("dp", "tensor"),
        P("dp", "tensor"),
        P("tensor", "dp"),
        P("tensor", "dp"),
    )
    return jax.shard_map(
        body,
        mesh=mesh,
        in_specs=placed,
        out_specs=(P("tensor", "dp"), P("tensor", "dp")),
        check_vma=False,
    )
```

```python
import jax
import jax.numpy as jnp
from jax import lax
from jax.sharding import Mesh, PartitionSpec as P

Y_HI, CORES, X = 2, 2, 4
DP = ("y_hi", "z")
TENSOR = ("x", "y_lo", "core")
SWAP = [(0, 1), (1, 0)]


def gather(block, axes):
    copies = jnp.broadcast_to(block[None], (lax.axis_size(axes), *block.shape))
    return lax.all_to_all(copies, axes, 0, 0, tiled=True)


def body(tokens, gate_weight, up_weight, down_weight, out_grad):
    hidden_width = gate_weight.shape[1]
    own_rows, width = tokens.shape
    layers, tensor = lax.axis_size("z"), lax.axis_size(TENSOR)
    rows = own_rows * tensor
    with jax.named_scope("gather_tokens"):
        both = gather(jnp.concatenate([tokens, out_grad]), ("x", "y_lo"))
        first = lax.axis_index("core") == 0

        def pair(mine):
            other = lax.ppermute(mine, "core", SWAP)
            ordered = [jnp.where(first, mine, other), jnp.where(first, other, mine)]
            return jnp.stack(ordered, axis=1).reshape(rows, width)

        gathered = pair(both[:, :own_rows])
        cotangent = pair(both[:, own_rows:])
    with jax.named_scope("gate_up_partial"):
        paired = jnp.concatenate([gate_weight, up_weight], axis=1)
        partial = jnp.dot(gathered, paired, preferred_element_type=jnp.float32)
        partial = partial.astype(jnp.bfloat16).reshape(layers, rows // layers, 2 * hidden_width)
    with jax.named_scope("gate_up_exchange"):
        parts = lax.all_to_all(partial, "z", 0, 0, tiled=True)
        half = parts.astype(jnp.float32).sum(axis=0)
        summed = half + lax.ppermute(half, "y_hi", SWAP)
    with jax.named_scope("activation"):
        share = jax.nn.silu(summed[:, :hidden_width]) * summed[:, hidden_width:]
        share = share.astype(jnp.bfloat16)
    with jax.named_scope("gather_hidden"):
        hidden = gather(share, "z").reshape(rows, hidden_width)
    with jax.named_scope("down"):
        mixed_partial = jnp.dot(hidden, down_weight, preferred_element_type=jnp.float32)
    with jax.named_scope("mixed_exchange"):
        mixed_partial = mixed_partial.astype(jnp.bfloat16).reshape(tensor, own_rows, width)
        mixed_parts = lax.all_to_all(mixed_partial, TENSOR, 0, 0, tiled=True)
        mixed = mixed_parts.astype(jnp.float32).sum(axis=0).astype(jnp.bfloat16)
    with jax.named_scope("down_grad"):
        contract = (((0,), (0,)), ((), ()))
        down_grad = lax.dot_general(hidden, cotangent, contract, preferred_element_type=jnp.float32)
    return (mixed, down_grad.astype(jnp.bfloat16))


def solution(mesh):
    dp, tensor = mesh.shape["dp"], mesh.shape["tensor"]
    sizes = (Y_HI, dp // Y_HI, X, tensor // (X * CORES), CORES)
    fine = Mesh(mesh.devices.reshape(sizes), (*DP, *TENSOR))
    placed = (P(TENSOR, DP), P(DP, TENSOR), P(DP, TENSOR), P(TENSOR, DP), P(TENSOR, DP))
    return jax.shard_map(
        body,
        mesh=fine,
        in_specs=placed,
        out_specs=(P(TENSOR, DP), P(TENSOR, DP)),
        check_vma=False,
    )
```

```python
import jax
import jax.numpy as jnp
from jax import lax
from jax.sharding import Mesh, PartitionSpec as P

Y_HI, CORES, X = 2, 2, 4
DP = ("y_hi", "z")
TENSOR = ("x", "y_lo", "core")
SWAP = [(0, 1), (1, 0)]


def gather(block, axes):
    copies = jnp.broadcast_to(block[None], (lax.axis_size(axes), *block.shape))
    return lax.all_to_all(copies, axes, 0, 0, tiled=True)


def body(tokens, gate_weight, up_weight, down_weight, out_grad):
    hidden_width = gate_weight.shape[1]
    own_rows, width = tokens.shape
    layers, chips = lax.axis_size("z"), lax.axis_size(("x", "y_lo"))
    rows = own_rows * chips * CORES
    with jax.named_scope("gather_tokens"):
        mine = gather(jnp.concatenate([tokens, out_grad]), ("x", "y_lo"))
        both = jnp.stack([mine, lax.ppermute(mine, "core", SWAP)])
        gathered = both[:, :, :own_rows].reshape(rows, width)
        cotangent = both[:, :, own_rows:].reshape(rows, width)
    with jax.named_scope("gate_up_partial"):
        paired = jnp.concatenate([gate_weight, up_weight], axis=1)
        partial = jnp.dot(gathered, paired, preferred_element_type=jnp.float32)
        partial = partial.astype(jnp.bfloat16).reshape(layers, rows // layers, 2 * hidden_width)
    with jax.named_scope("gate_up_exchange"):
        parts = lax.all_to_all(partial, "z", 0, 0, tiled=True)
        half = parts.astype(jnp.float32).sum(axis=0)
        summed = half + lax.ppermute(half, "y_hi", SWAP)
    with jax.named_scope("activation"):
        share = jax.nn.silu(summed[:, :hidden_width]) * summed[:, hidden_width:]
        share = share.astype(jnp.bfloat16)
    with jax.named_scope("gather_hidden"):
        hidden = gather(share, "z").reshape(rows, hidden_width)
    with jax.named_scope("down"):
        mixed_partial = jnp.dot(hidden, down_weight, preferred_element_type=jnp.float32)
    with jax.named_scope("mixed_exchange"):
        kept, sent = mixed_partial[: rows // CORES], mixed_partial[rows // CORES :]
        chip_sum = kept + lax.ppermute(sent, "core", SWAP)
        chip_sum = chip_sum.astype(jnp.bfloat16).reshape(chips, own_rows, width)
        mixed_parts = lax.all_to_all(chip_sum, ("x", "y_lo"), 0, 0, tiled=True)
        mixed = mixed_parts.astype(jnp.float32).sum(axis=0).astype(jnp.bfloat16)
    with jax.named_scope("down_grad"):
        contract = (((0,), (0,)), ((), ()))
        down_grad = lax.dot_general(hidden, cotangent, contract, preferred_element_type=jnp.float32)
    return (mixed, down_grad.astype(jnp.bfloat16))


def solution(mesh):
    dp, tensor = mesh.shape["dp"], mesh.shape["tensor"]
    sizes = (Y_HI, dp // Y_HI, X, tensor // (X * CORES), CORES)
    fine = Mesh(mesh.devices.reshape(sizes), (*DP, *TENSOR))
    placed = (P(TENSOR, DP), P(DP, TENSOR), P(DP, TENSOR), P(TENSOR, DP), P(TENSOR, DP))
    return jax.shard_map(
        body,
        mesh=fine,
        in_specs=placed,
        out_specs=(P(TENSOR, DP), P(TENSOR, DP)),
        check_vma=False,
    )
```

```python
import jax
import jax.numpy as jnp
from jax import lax
from jax.sharding import Mesh, PartitionSpec as P

Y_HI, CORES, X = 2, 2, 4
DP = ("y_hi", "z")
TENSOR = ("x", "y_lo", "core")
SWAP = [(0, 1), (1, 0)]


def gather(block, axes):
    copies = jnp.broadcast_to(block[None], (lax.axis_size(axes), *block.shape))
    return lax.all_to_all(copies, axes, 0, 0, tiled=True)


def body(tokens, gate_weight, up_weight, down_weight, out_grad):
    hidden_width = gate_weight.shape[1]
    own_rows, width = tokens.shape
    layers, chips = lax.axis_size("z"), lax.axis_size(("x", "y_lo"))
    rows = own_rows * chips * CORES
    with jax.named_scope("gather_tokens"):
        mine = gather(jnp.concatenate([tokens, out_grad]), ("x", "y_lo"))
        both = jnp.stack([mine, lax.ppermute(mine, "core", SWAP)])
        gathered = both[:, :, :own_rows].reshape(rows, width)
        cotangent = both[:, :, own_rows:].reshape(rows, width)
    with jax.named_scope("gate_up_partial"):
        paired = jnp.concatenate([gate_weight, up_weight], axis=1)
        partial = jnp.dot(gathered, paired, preferred_element_type=jnp.float32)
        partial = partial.astype(jnp.bfloat16).reshape(layers, rows // layers, 2 * hidden_width)
    with jax.named_scope("gate_up_exchange"):
        parts = lax.all_to_all(partial, "z", 0, 0, tiled=True)
        half = parts.astype(jnp.float32).sum(axis=0)
        summed = lax.all_gather(half, "y_hi").sum(axis=0)
    with jax.named_scope("activation"):
        share = jax.nn.silu(summed[:, :hidden_width]) * summed[:, hidden_width:]
        share = share.astype(jnp.bfloat16)
    with jax.named_scope("gather_hidden"):
        hidden = gather(share, "z").reshape(rows, hidden_width)
    with jax.named_scope("down"):
        mixed_partial = jnp.dot(hidden, down_weight, preferred_element_type=jnp.float32)
    with jax.named_scope("mixed_exchange"):
        kept, sent = mixed_partial[: rows // CORES], mixed_partial[rows // CORES :]
        chip_sum = kept + lax.dynamic_index_in_dim(
            lax.all_gather(sent, "core"), 1 - lax.axis_index("core"), 0, keepdims=False
        )
        chip_sum = chip_sum.astype(jnp.bfloat16).reshape(chips, own_rows, width)
        mixed_parts = lax.all_to_all(chip_sum, ("x", "y_lo"), 0, 0, tiled=True)
        mixed = mixed_parts.astype(jnp.float32).sum(axis=0).astype(jnp.bfloat16)
    with jax.named_scope("down_grad"):
        contract = (((0,), (0,)), ((), ()))
        down_grad = lax.dot_general(hidden, cotangent, contract, preferred_element_type=jnp.float32)
    return (mixed, down_grad.astype(jnp.bfloat16))


def solution(mesh):
    dp, tensor = mesh.shape["dp"], mesh.shape["tensor"]
    sizes = (Y_HI, dp // Y_HI, X, tensor // (X * CORES), CORES)
    fine = Mesh(mesh.devices.reshape(sizes), (*DP, *TENSOR))
    placed = (P(TENSOR, DP), P(DP, TENSOR), P(DP, TENSOR), P(TENSOR, DP), P(TENSOR, DP))
    return jax.shard_map(
        body,
        mesh=fine,
        in_specs=placed,
        out_specs=(P(TENSOR, DP), P(TENSOR, DP)),
        check_vma=False,
    )
```
